512 devices in a mesh: slab: 64 (over x, z, core), head: 8 (over y).
Axes of the slice: x: 4, y: 8, z: 8, core: 2. Of those that a mesh axis runs over, the one named last changes fastest.
Arguments:
- queries: bfloat16 [16384, 4096], P('slab', 'head'), may hold values from -12 to 12, as said below
- keys: bfloat16 [16384, 2048], P('slab', 'head'), may hold values from -4 to 4
- values: bfloat16 [16384, 2048], P('slab', 'head'), may hold values from -5 to 5
- user_lengths: int32 [4], replicated, may hold values from 1 to 8192, 16384 in all
- page_slot: int32 [1024], replicated, may hold values from 0 to 1023, as said below
Outputs:
- attention_out: bfloat16 [16384, 4096], P(('slab', 'head'))
- kv_cache: bfloat16 [1024, 2, 16, 2048], P('slab', None, None, 'head')
The draws below stay inside these ranges and needn't reach their ends.
Inputs may be any that keep to these rules, and one draw needn't show every extreme that they name: `queries`: entries are shaped as normal activations; the ends of the range are reached only by a few rows. `user_lengths`: every history has at least one token, they sum to 16384, and the longest has exactly 8192. `page_slot`: A permutation of the 1024 slots; slot s is held by slab index s // 16. The 16 pages of one slab go to 16 different slab indices, one slot each.
All inputs are finite; a program needn't handle non-finite values.
Results may differ from the reference program's by a relative error of at most 0.0042.
Values may be sent and summed in bfloat16 or wider, within the bound.
No kernel may reach another device: no remote copies, remote signals or barrier semaphores. Data moves between devices by JAX's collectives and lax.ppermute only.
A program may use at most 64 MiB of HBM per device.

```python
import math
import jax
import jax.numpy as jnp
import numpy as np
from jax import lax

HEADS = 32
KV_HEADS = 16
HEAD_DIM = 128
WINDOW = 1024
PAGE_ROWS = 16
TOKENS = 16384
USERS = 4
LONGEST = 8192
PAGES = 1024
PAGES_DEV = 16
N_SLAB = 64


def draw_keys(key, part):
    key = jax.random.fold_in(key, 3)
    result = jnp.clip(jax.random.normal(key, (TOKENS, KV_HEADS * HEAD_DIM)), -4.0, 4.0)
    return result.astype(jnp.bfloat16)


def draw_queries(key, part):
    key = jax.random.fold_in(key, 7)
    result = jnp.clip(jax.random.normal(key, (TOKENS, HEADS * HEAD_DIM)), -4.0, 4.0)
    return result.astype(jnp.bfloat16)


def draw_page_slot(key, part):
    key = jax.random.fold_in(key, 11)
    slab_key, local_key, owner_key = jax.random.split(key, 3)
    slab_order = jax.random.permutation(slab_key, N_SLAB).astype(jnp.int32)
    local_order = jax.random.permutation(local_key, PAGES_DEV).astype(jnp.int32)
    summed = slab_order[:, None] + local_order[None, :]
    target_owner = N_SLAB // 2 - 1
    offset = (target_owner - summed[N_SLAB - 1, PAGES_DEV - 1] % N_SLAB + N_SLAB) % N_SLAB
    owners = (summed + offset) % N_SLAB
    owner_orders = jax.vmap(lambda each_key: jax.random.permutation(each_key, PAGES_DEV))(jax.random.split(owner_key, N_SLAB))
    local_slots = owner_orders[owners, jnp.arange(PAGES_DEV)[None, :]]
    return (owners * PAGES_DEV + local_slots).reshape(PAGES).astype(jnp.int32)


def block_scale(rng, extent, cuts, smallest, high):
    def one(dim, parts):
        steps = jax.random.uniform(jax.random.fold_in(jax.random.fold_in(rng, 6), dim), (parts,), jnp.float32, smallest / len(cuts), high / len(cuts))
        return jnp.repeat(jnp.exp(steps), extent[dim] // parts).reshape((-1,) + (1,) * (len(extent) - dim - 1))

    gain = one(*cuts[0])
    for cut in cuts[1:]:
        gain = gain * one(*cut)
    return gain


def profile(number_of, total, limit, lean):
    portions = [(1 << 20) // math.isqrt(grade ** lean) + 1 for grade in range(2, number_of + 1)]
    spare, counts = total - limit - (number_of - 1), [1] * (number_of - 1)
    while spare > 0:
        movable = [i for i in range(number_of - 1) if counts[i] < limit]
        whole, budget = sum([portions[i] for i in movable]), spare
        for i in movable:
            extra = min(limit - counts[i], max(1, budget * portions[i] // whole), spare)
            counts[i] = counts[i] + extra
            spare = spare - extra
    return np.array([limit] + counts)


def uneven(key, amount, total, reach, slope):
    if amount == 2:
        one = jax.random.randint(key, (), max(1, total - reach), min(reach, total - 1) + 1)
        return jnp.stack([one, total - one])
    tallies = jnp.asarray(profile(amount, total, reach, slope), jnp.int32)
    pairs = (amount - 1) // 2
    donor, taker = tallies[1:1 + 2 * pairs:2], tallies[2:2 + 2 * pairs:2]
    room = jnp.minimum(donor - 1, reach - taker)
    passed = jax.random.randint(jax.random.fold_in(key, 1), (pairs,), 0, 1 << 20) % (room + 1)
    tallies = tallies.at[1:1 + 2 * pairs:2].set(donor - passed).at[2:2 + 2 * pairs:2].set(taker + passed)
    return tallies[jax.random.permutation(jax.random.fold_in(key, 2), amount)]


def noise(rng, extent, scale, bound, pieces=(), kind=jnp.bfloat16):
    entries = scale * jax.random.normal(rng, extent, jnp.float32)
    if pieces:
        entries = entries * block_scale(rng, extent, pieces, -0.22, 0.18)
    return jnp.clip(entries, -bound, bound).astype(kind)


def setup_inputs(seed: int = 0) -> dict:
    seeds = jax.random.split(jax.random.key(seed), 6)
    queries = draw_queries(jax.random.fold_in(seeds[5], 71), 0)
    keys = draw_keys(jax.random.fold_in(seeds[5], 71), 0)
    values = noise(seeds[2], (TOKENS, KV_HEADS * HEAD_DIM), 1.0, 5.0, ((0, 64), (1, 8)))
    user_lengths = uneven(seeds[3], USERS, TOKENS, LONGEST, 2).astype(jnp.int32)
    page_slot = draw_page_slot(jax.random.fold_in(seeds[5], 71), 0)
    return dict(queries=queries, keys=keys, values=values, user_lengths=user_lengths, page_slot=page_slot)


QUERY_SCALE = 168.0 ** -0.5
MASKED = -1.0e30


def bounds(positions, user_lengths):
    user_ends = jnp.cumsum(user_lengths).astype(jnp.int32)
    user_starts = (user_ends - user_lengths).astype(jnp.int32)
    user_first = jnp.max(jnp.where(user_starts[None, :] <= positions[:, None], user_starts[None, :], 0), axis=1)
    user_last = jnp.min(jnp.where(user_ends[None, :] > positions[:, None], user_ends[None, :], user_ends[-1]), axis=1)
    return user_first.astype(jnp.int32), user_last.astype(jnp.int32)


def attend(query_rows, key_rows, value_rows, query_pos, key_pos, query_first):
    row_count = query_rows.shape[0]
    group_size = HEADS // KV_HEADS
    query_heads = query_rows.astype(jnp.float32).reshape(row_count, KV_HEADS, group_size, HEAD_DIM)
    key_heads = key_rows.astype(jnp.float32).reshape(-1, KV_HEADS, HEAD_DIM)
    value_heads = value_rows.astype(jnp.float32).reshape(-1, KV_HEADS, HEAD_DIM)
    scores = jnp.einsum("qgrd,kgd->grqk", query_heads, key_heads) * QUERY_SCALE
    allowed = (key_pos[None, :] >= query_first[:, None]) & (key_pos[None, :] <= query_pos[:, None]) & (query_pos[:, None] - key_pos[None, :] < WINDOW)
    scores = jnp.where(allowed[None, None], scores, MASKED)
    row_max = jnp.max(scores, axis=-1, keepdims=True)
    shifted = jnp.where(allowed[None, None], jnp.exp(scores - row_max), 0.0)
    denominators = jnp.sum(shifted, axis=-1)
    weights = lax.optimization_barrier(shifted.astype(jnp.bfloat16))
    mixed = jnp.einsum("grqk,kgd->grqd", weights.astype(jnp.float32), value_heads) / denominators[..., None]
    return jnp.transpose(mixed, (2, 0, 1, 3)).reshape(row_count, HEADS * HEAD_DIM).astype(jnp.bfloat16)


def reference(queries, keys, values, user_lengths, page_slot):
    block_rows = math.gcd(512, TOKENS)
    block_count = TOKENS // block_rows
    kv_width = KV_HEADS * HEAD_DIM
    padded_keys = jnp.concatenate([jnp.zeros((WINDOW, kv_width), keys.dtype), keys], axis=0)
    padded_values = jnp.concatenate([jnp.zeros((WINDOW, kv_width), values.dtype), values], axis=0)

    def attend_block(block_index):
        block_start = (block_index * block_rows).astype(jnp.int32)
        query_rows = lax.dynamic_slice_in_dim(queries, block_start, block_rows, 0)
        key_rows = lax.dynamic_slice_in_dim(padded_keys, block_start, WINDOW + block_rows, 0)
        value_rows = lax.dynamic_slice_in_dim(padded_values, block_start, WINDOW + block_rows, 0)
        query_pos = block_start + jnp.arange(block_rows, dtype=jnp.int32)
        key_pos = block_start - WINDOW + jnp.arange(WINDOW + block_rows, dtype=jnp.int32)
        query_first, unused_last = bounds(query_pos, user_lengths)
        return attend(query_rows, key_rows, value_rows, query_pos, key_pos, query_first)

    attention_out = lax.map(attend_block, jnp.arange(block_count, dtype=jnp.int32)).reshape(TOKENS, HEADS * HEAD_DIM)

    positions = jnp.arange(TOKENS, dtype=jnp.int32)
    unused_first, user_last = bounds(positions, user_lengths)
    live = positions >= user_last - WINDOW
    key_pages = jnp.where(live[:, None], keys, jnp.zeros_like(keys)).reshape(PAGES, PAGE_ROWS, kv_width)
    value_pages = jnp.where(live[:, None], values, jnp.zeros_like(values)).reshape(PAGES, PAGE_ROWS, kv_width)
    page_data = jnp.stack([key_pages, value_pages], axis=1)
    kv_cache = jnp.zeros_like(page_data).at[page_slot].set(page_data)
    return attention_out, kv_cache
```

```python
import functools

import jax
import jax.numpy as jnp
from jax import lax
from jax.experimental import pallas as pl
from jax.experimental.pallas import tpu as pltpu
from jax.sharding import Mesh
from jax.sharding import PartitionSpec as P

HEAD_DIM = 128
WINDOW = 1024
PAGE_ROWS = 16
QUERY_SCALE = 168.0 ** (-0.5)
LOG2_E = 1.4426950408889634
MASKED = -1e30
CORES = 2
ATTEND_WEIGHT = 22

VMEM = pl.BlockSpec(memory_space=pltpu.VMEM)
SMEM = pl.BlockSpec(memory_space=pltpu.SMEM)
ANY = pl.BlockSpec(memory_space=pl.ANY)


def user_first(positions, lengths_ref):
    first = jnp.zeros_like(positions)
    start = jnp.int32(0)
    for user in range(lengths_ref.shape[0]):
        first = jnp.where(positions >= start, start, first)
        start = start + lengths_ref[user]
    return first


def user_last(positions, lengths_ref):
    ends = []
    end = jnp.int32(0)
    for user in range(lengths_ref.shape[0]):
        end = end + lengths_ref[user]
        ends.append(end)
    last = jnp.zeros_like(positions) + ends[-1]
    for end in reversed(ends[:-1]):
        last = jnp.where(positions < end, end, last)
    return last


def pages_kernel(place_ref, lengths_ref, slot_ref, own_ref, out_ref):
    slab = place_ref[0]
    tokens, kv_width = own_ref.shape[1:]
    pages = tokens // PAGE_ROWS
    out_ref[...] = jnp.zeros_like(out_ref)
    for page in range(pages):
        rows = slice(page * PAGE_ROWS, (page + 1) * PAGE_ROWS)
        positions = (slab * pages + page) * PAGE_ROWS + lax.broadcasted_iota(
            jnp.int32, (PAGE_ROWS, kv_width), 0
        )
        live = positions >= user_last(positions, lengths_ref) - WINDOW
        owner = slot_ref[slab * pages + page] // pages
        for side in range(2):
            out_ref[owner, side] = jnp.where(live, own_ref[side, rows, :], 0).astype(out_ref.dtype)


def collect_kernel(source_ref, in_ref, out_ref, sems):
    copies = [
        pltpu.make_async_copy(in_ref.at[source_ref[slot]], out_ref.at[slot], sems.at[slot])
        for slot in range(out_ref.shape[0])
    ]
    for copy in copies:
        copy.start()
    for copy in copies:
        copy.wait()


def attend_kernel(
    place_ref, lengths_ref, queries_ref, own_ref, near_ref, far_ref, partner_ref, out_ref
):
    slab, core = place_ref[0], place_ref[1]
    tokens = queries_ref.shape[0]
    kv_local = own_ref.shape[2] // HEAD_DIM
    group = queries_ref.shape[1] // (kv_local * HEAD_DIM)
    first_core = core == 0
    pieces = [
        (own_ref, 0),
        (near_ref, 2),
        (far_ref, 4),
        (partner_ref.at[0], jnp.where(first_core, 1, 3)),
        (partner_ref.at[1], jnp.where(first_core, 3, 1)),
    ]
    row = lax.broadcasted_iota(jnp.int32, (tokens, 1), 0)
    column = lax.broadcasted_iota(jnp.int32, (tokens, tokens), 1)
    first = user_first(slab * tokens + row, lengths_ref)
    causal = column <= lax.broadcasted_iota(jnp.int32, (tokens, tokens), 0)
    for g in range(kv_local):
        kv_columns = slice(g * HEAD_DIM, (g + 1) * HEAD_DIM)
        for r in range(group):
            h = g * group + r
            query = queries_ref[:, h * HEAD_DIM : (h + 1) * HEAD_DIM]
            scores = []
            for ref, back in pieces:
                s = lax.dot_general(
                    query,
                    ref[0, :, kv_columns],
                    (((1,), (1,)), ((), ())),
                    preferred_element_type=jnp.float32,
                )
                begin = first - (slab - back) * tokens
                if ref is far_ref:
                    begin = jnp.maximum(begin, row + 1)
                allowed = column >= begin
                if ref is own_ref:
                    allowed = allowed & causal
                scores.append(jnp.where(allowed, s, MASKED))
            peak = functools.reduce(jnp.maximum, scores)
            row_max = jnp.max(peak, axis=1, keepdims=True)
            total, mixed = None, None
            for (ref, back), s in zip(pieces, scores):
                shifted = jnp.exp2((s - row_max) * (QUERY_SCALE * LOG2_E))
                part = jnp.dot(
                    shifted.astype(jnp.bfloat16),
                    ref[1, :, kv_columns],
                    preferred_element_type=jnp.float32,
                )
                total = shifted if total is None else total + shifted
                mixed = part if mixed is None else mixed + part
            denominators = jnp.sum(total, axis=1, keepdims=True)
            out_ref[:, h * HEAD_DIM : (h + 1) * HEAD_DIM] = (mixed / denominators).astype(
                out_ref.dtype
            )


def cost(flops, moved):
    return pl.CostEstimate(flops=flops, bytes_accessed=moved, transcendentals=0)


def body(queries, keys, values, user_lengths, page_slot):
    slab_axes = ("x", "z", "core")
    tokens, kv_width = keys.shape
    slabs = page_slot.shape[0] // (tokens // PAGE_ROWS)
    pages = tokens // PAGE_ROWS
    slab = lax.axis_index(slab_axes)
    core = lax.axis_index("core")
    place = jnp.stack([slab, core]).astype(jnp.int32)

    own = jnp.stack([keys, values])
    outgoing = pl.pallas_call(
        pages_kernel,
        out_shape=jax.ShapeDtypeStruct((slabs, 2, PAGE_ROWS, kv_width), jnp.bfloat16),
        in_specs=[SMEM, SMEM, SMEM, VMEM],
        out_specs=VMEM,
        cost_estimate=cost(0, slabs * pages * PAGE_ROWS * kv_width * 4),
        name="pages",
    )(place, user_lengths, page_slot, own)
    incoming = lax.all_to_all(outgoing, slab_axes, split_axis=0, concat_axis=0, tiled=True)
    chips = lax.axis_size("x") * lax.axis_size("z")
    near, far = [
        lax.ppermute(own, ("x", "z"), [(i, i + hop) for i in range(chips - hop)])
        for hop in (1, 2)
    ]
    given = jnp.stack([near, jnp.where(core == 0, own, far)])
    partner = lax.ppermute(given, "core", [(0, 1), (1, 0)])

    slots = slab * pages + jnp.arange(pages, dtype=jnp.int32)
    page_index = jnp.arange(page_slot.shape[0], dtype=jnp.int32)
    source = jnp.sum(
        jnp.where(page_slot[None, :] == slots[:, None], page_index[None, :] // pages, 0), axis=1
    )

    attended = pl.pallas_call(
        attend_kernel,
        out_shape=jax.ShapeDtypeStruct(queries.shape, jnp.bfloat16),
        in_specs=[SMEM, SMEM, VMEM, VMEM, VMEM, VMEM, VMEM],
        out_specs=VMEM,
        cost_estimate=cost(ATTEND_WEIGHT * 4 * queries.shape[0] * queries.shape[1] * 5 * tokens, 2 << 20),
        compiler_params=pltpu.CompilerParams(vmem_limit_bytes=24 << 20),
        name="attend",
    )(place, user_lengths, queries, own, near, far, partner)
    attended, incoming = lax.optimization_barrier((attended, incoming))
    attention_out = lax.all_to_all(attended, "head", split_axis=0, concat_axis=1, tiled=True)

    kv_cache = pl.pallas_call(
        collect_kernel,
        out_shape=jax.ShapeDtypeStruct((pages, 2, PAGE_ROWS, kv_width), jnp.bfloat16),
        in_specs=[SMEM, ANY],
        out_specs=VMEM,
        scratch_shapes=[pltpu.SemaphoreType.DMA((pages,))],
        cost_estimate=cost(0, pages * PAGE_ROWS * kv_width * 8),
        name="collect",
    )(source, incoming)
    return attention_out, kv_cache


def solution(mesh):
    x, z, y = 4, 8, mesh.shape["head"]
    chips = mesh.shape["slab"] // CORES
    z = next(n for n in (8, 4, 2, 1) if chips % n == 0)
    x = chips // z
    split = Mesh(mesh.devices.reshape(x, z, CORES, y), ("x", "z", "core", "head"))
    return jax.shard_map(
        body,
        mesh=split,
        in_specs=(
            P(("x", "z", "core"), "head"),
            P(("x", "z", "core"), "head"),
            P(("x", "z", "core"), "head"),
            P(),
            P(),
        ),
        out_specs=(
            P(("x", "z", "core", "head"), None),
            P(("x", "z", "core"), None, None, "head"),
        ),
        check_vma=False,
    )
```

```python
import functools

import jax
import jax.numpy as jnp
from jax import lax
from jax.experimental import pallas as pl
from jax.experimental.pallas import tpu as pltpu
from jax.sharding import Mesh
from jax.sharding import PartitionSpec as P

HEAD_DIM = 128
WINDOW = 1024
PAGE_ROWS = 16
QUERY_SCALE = 168.0 ** (-0.5)
LOG2_E = 1.4426950408889634
MASKED = -1e30
CORES = 2
HALVES = 2
ATTEND_WEIGHT = 14

VMEM = pl.BlockSpec(memory_space=pltpu.VMEM)
SMEM = pl.BlockSpec(memory_space=pltpu.SMEM)
ANY = pl.BlockSpec(memory_space=pl.ANY)


def user_first(positions, lengths_ref):
    first = jnp.zeros_like(positions)
    start = jnp.int32(0)
    for user in range(lengths_ref.shape[0]):
        first = jnp.where(positions >= start, start, first)
        start = start + lengths_ref[user]
    return first


def user_last(positions, lengths_ref):
    ends = []
    end = jnp.int32(0)
    for user in range(lengths_ref.shape[0]):
        end = end + lengths_ref[user]
        ends.append(end)
    last = jnp.zeros_like(positions) + ends[-1]
    for end in reversed(ends[:-1]):
        last = jnp.where(positions < end, end, last)
    return last


def here():
    core = lax.axis_index("core")
    chip = lax.axis_index("x") * lax.axis_size("z") + lax.axis_index("z")
    return chip * CORES + core, core


def prepare_kernel(lengths_ref, slot_ref, keys_ref, values_ref, out_ref, live_ref, sems):
    slab, _ = here()
    tokens, kv_width = keys_ref.shape
    pages = tokens // PAGE_ROWS
    copies = []
    for page in range(pages):
        rows = slice(page * PAGE_ROWS, (page + 1) * PAGE_ROWS)
        positions = (slab * pages + page) * PAGE_ROWS + lax.broadcasted_iota(
            jnp.int32, (PAGE_ROWS, kv_width), 0
        )
        live = positions >= user_last(positions, lengths_ref) - WINDOW
        for side, ref in enumerate((keys_ref, values_ref)):
            live_ref[page, side] = jnp.where(live, ref[rows, :], 0).astype(live_ref.dtype)
        owner = slot_ref[slab * pages + page] // pages
        copies.append(pltpu.make_async_copy(live_ref.at[page], out_ref.at[owner], sems.at[page]))
        copies[-1].start()
    for copy in copies:
        copy.wait()


def collect_kernel(source_ref, in_ref, out_ref):
    for slot in range(out_ref.shape[0]):
        out_ref[slot] = in_ref[source_ref[slot]]


def attend_kernel(
    lengths_ref, queries_ref, own_ref, near_ref, far_ref, partner_ref, kept_ref, sent_ref
):
    slab, core = here()
    tokens = queries_ref.shape[0]
    kv_local = own_ref.shape[2] // HEAD_DIM
    group = queries_ref.shape[1] // (kv_local * HEAD_DIM)
    first_core = core == 0
    first_half = lax.axis_index("half") == 0
    pieces = [
        (own_ref, 0),
        (near_ref, 2),
        (far_ref, 4),
        (partner_ref.at[0], jnp.where(first_core, 1, 3)),
        (partner_ref.at[1], jnp.where(first_core, 3, 1)),
    ]
    row = lax.broadcasted_iota(jnp.int32, (tokens, 1), 0)
    column = lax.broadcasted_iota(jnp.int32, (tokens, tokens), 1)
    first = user_first(slab * tokens + row, lengths_ref)
    causal = column <= lax.broadcasted_iota(jnp.int32, (tokens, tokens), 0)
    for g in range(kv_local):
        kv_columns = slice(g * HEAD_DIM, (g + 1) * HEAD_DIM)
        for r in range(group):
            h = g * group + r
            query = queries_ref[:, h * HEAD_DIM : (h + 1) * HEAD_DIM]
            scores = []
            for ref, back in pieces:
                s = lax.dot_general(
                    query,
                    ref[0, :, kv_columns],
                    (((1,), (1,)), ((), ())),
                    preferred_element_type=jnp.float32,
                )
                begin = first - (slab - back) * tokens
                if ref is far_ref:
                    begin = jnp.maximum(begin, row + 1)
                allowed = column >= begin
                if ref is own_ref:
                    allowed = allowed & causal
                scores.append(jnp.where(allowed, s, MASKED))
            peak = functools.reduce(jnp.maximum, scores)
            row_max = jnp.max(peak, axis=1, keepdims=True)
            total, mixed = None, None
            for (ref, back), s in zip(pieces, scores):
                shifted = jnp.exp2((s - row_max) * (QUERY_SCALE * LOG2_E))
                part = jnp.dot(
                    shifted.astype(jnp.bfloat16),
                    ref[1, :, kv_columns],
                    preferred_element_type=jnp.float32,
                )
                total = shifted if total is None else total + shifted
                mixed = part if mixed is None else mixed + part
            denominators = jnp.sum(total, axis=1, keepdims=True)
            result = (mixed / denominators).astype(kept_ref.dtype)
            lower, upper = result[: tokens // HALVES], result[tokens // HALVES :]
            columns = slice(h * HEAD_DIM, (h + 1) * HEAD_DIM)
            kept_ref[:, columns] = jnp.where(first_half, lower, upper)
            sent_ref[:, columns] = jnp.where(first_half, upper, lower)


def cost(flops, moved):
    return pl.CostEstimate(flops=flops, bytes_accessed=moved, transcendentals=0)


def body(queries, keys, values, user_lengths, page_slot):
    slab_axes = ("x", "z", "core")
    tokens, kv_width = keys.shape
    slabs = page_slot.shape[0] // (tokens // PAGE_ROWS)
    pages = tokens // PAGE_ROWS
    slab = lax.axis_index(slab_axes)
    core = lax.axis_index("core")

    page_block = (2, PAGE_ROWS, kv_width)
    own = jnp.stack([keys, values])
    outgoing = pl.pallas_call(
        prepare_kernel,
        out_shape=jax.ShapeDtypeStruct((slabs,) + page_block, jnp.bfloat16),
        in_specs=[SMEM, SMEM, VMEM, VMEM],
        out_specs=ANY,
        scratch_shapes=[
            pltpu.VMEM((pages,) + page_block, jnp.bfloat16),
            pltpu.SemaphoreType.DMA((pages,)),
        ],
        cost_estimate=cost(0, pages * PAGE_ROWS * kv_width * 16),
        name="prepare",
    )(user_lengths, page_slot, keys, values)
    incoming = lax.all_to_all(outgoing, slab_axes, split_axis=0, concat_axis=0, tiled=True)
    chips = lax.axis_size("x") * lax.axis_size("z")
    near, far = [
        lax.ppermute(own, ("x", "z"), [(i, i + hop) for i in range(chips - hop)])
        for hop in (1, 2)
    ]
    given = jnp.stack([near, jnp.where(core == 0, own, far)])
    swap = [(0, 1), (1, 0)]
    partner = lax.ppermute(given, "core", swap)

    slots = slab * pages + jnp.arange(pages, dtype=jnp.int32)
    page_index = jnp.arange(page_slot.shape[0], dtype=jnp.int32)
    source = jnp.sum(
        jnp.where(page_slot[None, :] == slots[:, None], page_index[None, :] // pages, 0), axis=1
    )

    half_rows = jax.ShapeDtypeStruct((tokens // HALVES, queries.shape[1]), jnp.bfloat16)
    kept, sent = pl.pallas_call(
        attend_kernel,
        out_shape=(half_rows, half_rows),
        in_specs=[SMEM, VMEM, VMEM, VMEM, VMEM, VMEM],
        out_specs=(VMEM, VMEM),
        cost_estimate=cost(
            ATTEND_WEIGHT * 4 * queries.shape[0] * queries.shape[1] * 5 * tokens, 2 << 20
        ),
        compiler_params=pltpu.CompilerParams(vmem_limit_bytes=16 << 20),
        name="attend",
    )(user_lengths, queries, own, near, far, partner)
    arrived = lax.ppermute(sent, "half", swap)
    first_half = lax.axis_index("half") == 0
    halves = [jnp.where(first_half, kept, arrived), jnp.where(first_half, arrived, kept)]
    quarters = lax.axis_size("quarter")
    attended = jnp.stack([part.reshape(quarters, -1, queries.shape[1]) for part in halves], axis=1)
    attended, incoming = lax.optimization_barrier((attended, incoming))
    exchanged = lax.all_to_all(attended, "quarter", split_axis=0, concat_axis=0, tiled=True)
    attention_out = jnp.transpose(exchanged, (2, 1, 0, 3)).reshape(exchanged.shape[2], -1)

    kv_cache = pl.pallas_call(
        collect_kernel,
        out_shape=jax.ShapeDtypeStruct((pages,) + page_block, jnp.bfloat16),
        in_specs=[SMEM, VMEM],
        out_specs=VMEM,
        cost_estimate=cost(0, pages * PAGE_ROWS * kv_width * 8),
        compiler_params=pltpu.CompilerParams(vmem_limit_bytes=4 << 20),
        name="collect",
    )(source, incoming)
    return attention_out, kv_cache


def solution(mesh):
    x, z, y = 4, 8, mesh.shape["head"]
    chips = mesh.shape["slab"] // CORES
    z = next(n for n in (8, 4, 2, 1) if chips % n == 0)
    x = chips // z
    axes = ("x", "z", "core", "half", "quarter")
    split = Mesh(mesh.devices.reshape(x, z, CORES, HALVES, y // HALVES), axes)
    slab, head = axes[:3], axes[3:]
    return jax.shard_map(
        body,
        mesh=split,
        in_specs=(P(slab, head), P(slab, head), P(slab, head), P(), P()),
        out_specs=(P(slab + head, None), P(slab, None, None, head)),
        check_vma=False,
    )
```

```python
import functools

import jax
import jax.numpy as jnp
from jax import lax
from jax.experimental import pallas as pl
from jax.experimental.pallas import tpu as pltpu
from jax.sharding import Mesh
from jax.sharding import PartitionSpec as P

HEAD_DIM = 128
WINDOW = 1024
PAGE_ROWS = 16
QUERY_SCALE = 168.0 ** (-0.5)
LOG2_E = 1.4426950408889634
MASKED = -1e30
CORES = 2
HALVES = 2
ATTEND_WEIGHT = 17

VMEM = pl.BlockSpec(memory_space=pltpu.VMEM)
SMEM = pl.BlockSpec(memory_space=pltpu.SMEM)
ANY = pl.BlockSpec(memory_space=pl.ANY)


def user_first(positions, lengths_ref):
    first = jnp.zeros_like(positions)
    start = jnp.int32(0)
    for user in range(lengths_ref.shape[0]):
        first = jnp.where(positions >= start, start, first)
        start = start + lengths_ref[user]
    return first


def user_last(positions, lengths_ref):
    ends = []
    end = jnp.int32(0)
    for user in range(lengths_ref.shape[0]):
        end = end + lengths_ref[user]
        ends.append(end)
    last = jnp.zeros_like(positions) + ends[-1]
    for end in reversed(ends[:-1]):
        last = jnp.where(positions < end, end, last)
    return last


def here():
    core = lax.axis_index("core")
    chip = lax.axis_index("x") * lax.axis_size("z") + lax.axis_index("z")
    return chip * CORES + core, core


def prepare_kernel(lengths_ref, slot_ref, keys_ref, values_ref, out_ref, live_ref, sems):
    slab, _ = here()
    tokens, kv_width = keys_ref.shape
    pages = tokens // PAGE_ROWS
    copies = []
    for page in range(pages):
        rows = slice(page * PAGE_ROWS, (page + 1) * PAGE_ROWS)
        positions = (slab * pages + page) * PAGE_ROWS + lax.broadcasted_iota(
            jnp.int32, (PAGE_ROWS, kv_width), 0
        )
        live = positions >= user_last(positions, lengths_ref) - WINDOW
        for side, ref in enumerate((keys_ref, values_ref)):
            live_ref[page, side] = jnp.where(live, ref[rows, :], 0).astype(live_ref.dtype)
        owner = slot_ref[slab * pages + page] // pages
        copies.append(pltpu.make_async_copy(live_ref.at[page], out_ref.at[owner], sems.at[page]))
        copies[-1].start()
    for copy in copies:
        copy.wait()


def collect_kernel(source_ref, in_ref, out_ref):
    for slot in range(out_ref.shape[0]):
        out_ref[slot] = in_ref[source_ref[slot]]


def attend_kernel(
    mine, lengths_ref, queries_ref, own_ref, near_ref, far_ref, partner_ref, out_ref, parts_ref
):
    slab, core = here()
    tokens = queries_ref.shape[0]
    kv_local = own_ref.shape[2] // HEAD_DIM
    group = queries_ref.shape[1] // (kv_local * HEAD_DIM)
    first_core = core == 0
    half, quarter = lax.axis_index("half"), lax.axis_index("quarter")
    quarters, part_rows = out_ref.shape[:2]
    rows = quarters * part_rows
    row_start = pl.multiple_of((half if mine else 1 - half) * rows, rows)
    pieces = [
        (own_ref, 0),
        (near_ref, 2),
        (far_ref, 4),
        (partner_ref.at[0], jnp.where(first_core, 1, 3)),
        (partner_ref.at[1], jnp.where(first_core, 3, 1)),
    ]
    row = row_start + lax.broadcasted_iota(jnp.int32, (rows, 1), 0)
    column = lax.broadcasted_iota(jnp.int32, (rows, tokens), 1)
    first = user_first(slab * tokens + row, lengths_ref)
    causal = column <= row
    for g in range(kv_local):
        kv_columns = slice(g * HEAD_DIM, (g + 1) * HEAD_DIM)
        for r in range(group):
            h = g * group + r
            query = queries_ref[pl.ds(row_start, rows), h * HEAD_DIM : (h + 1) * HEAD_DIM]
            scores = []
            for ref, back in pieces:
                s = lax.dot_general(
                    query,
                    ref[0, :, kv_columns],
                    (((1,), (1,)), ((), ())),
                    preferred_element_type=jnp.float32,
                )
                begin = first - (slab - back) * tokens
                if ref is far_ref:
                    begin = jnp.maximum(begin, row + 1)
                allowed = column >= begin
                if ref is own_ref:
                    allowed = allowed & causal
                scores.append(jnp.where(allowed, s, MASKED))
            peak = functools.reduce(jnp.maximum, scores)
            row_max = jnp.max(peak, axis=1, keepdims=True)
            total, mixed = None, None
            for (ref, back), s in zip(pieces, scores):
                shifted = jnp.exp2((s - row_max) * (QUERY_SCALE * LOG2_E))
                part = jnp.dot(
                    shifted.astype(jnp.bfloat16),
                    ref[1, :, kv_columns],
                    preferred_element_type=jnp.float32,
                )
                total = shifted if total is None else total + shifted
                mixed = part if mixed is None else mixed + part
            denominators = jnp.sum(total, axis=1, keepdims=True)
            result = (mixed / denominators).astype(out_ref.dtype)
            columns = slice(h * HEAD_DIM, (h + 1) * HEAD_DIM)
            for target in range(quarters):
                parts_ref[target, :, columns] = result[
                    target * part_rows : (target + 1) * part_rows
                ]
    for e in range(quarters):
        out_ref[e] = parts_ref[quarter ^ e]


def pair_kernel(kept_ref, arrived_ref, *out_refs):
    half = lax.axis_index("half")
    for e, ref in enumerate(out_refs):
        ref[half] = kept_ref[e]
        ref[1 - half] = arrived_ref[e]


def join_kernel(*refs):
    *in_refs, out_ref = refs
    quarter = lax.axis_index("quarter")
    width = in_refs[0].shape[2]
    for e, ref in enumerate(in_refs):
        for half in range(HALVES):
            start = (half * len(in_refs) + (quarter ^ e)) * width
            out_ref[:, pl.ds(pl.multiple_of(start, width), width)] = ref[half]


def cost(flops, moved):
    return pl.CostEstimate(flops=flops, bytes_accessed=moved, transcendentals=0)


def body(queries, keys, values, user_lengths, page_slot):
    slab_axes = ("x", "z", "core")
    tokens, kv_width = keys.shape
    slabs = page_slot.shape[0] // (tokens // PAGE_ROWS)
    pages = tokens // PAGE_ROWS
    slab = lax.axis_index(slab_axes)
    core = lax.axis_index("core")

    page_block = (2, PAGE_ROWS, kv_width)
    own = jnp.stack([keys, values])
    outgoing = pl.pallas_call(
        prepare_kernel,
        out_shape=jax.ShapeDtypeStruct((slabs,) + page_block, jnp.bfloat16),
        in_specs=[SMEM, SMEM, VMEM, VMEM],
        out_specs=ANY,
        scratch_shapes=[
            pltpu.VMEM((pages,) + page_block, jnp.bfloat16),
            pltpu.SemaphoreType.DMA((pages,)),
        ],
        cost_estimate=cost(0, pages * PAGE_ROWS * kv_width * 16),
        name="prepare",
    )(user_lengths, page_slot, keys, values)
    chips = lax.axis_size("x") * lax.axis_size("z")
    forward = [(i, i + 1) for i in range(chips - 1)]
    near = lax.ppermute(own, ("x", "z"), forward)
    near, outgoing = lax.optimization_barrier((near, outgoing))
    far = lax.ppermute(near, ("x", "z"), forward)
    incoming = lax.all_to_all(outgoing, slab_axes, split_axis=0, concat_axis=0, tiled=True)
    given = jnp.stack([near, jnp.where(core == 0, own, far)])
    swap = [(0, 1), (1, 0)]
    partner = lax.ppermute(given, "core", swap)

    slots = slab * pages + jnp.arange(pages, dtype=jnp.int32)
    page_index = jnp.arange(page_slot.shape[0], dtype=jnp.int32)
    source = jnp.sum(
        jnp.where(page_slot[None, :] == slots[:, None], page_index[None, :] // pages, 0), axis=1
    )

    quarters = lax.axis_size("quarter")
    part_rows = tokens // (HALVES * quarters)
    parts = jax.ShapeDtypeStruct((quarters, part_rows, queries.shape[1]), jnp.bfloat16)
    pair = jax.ShapeDtypeStruct((HALVES,) + parts.shape[1:], jnp.bfloat16)
    sent, kept = [
        pl.pallas_call(
            functools.partial(attend_kernel, mine),
            out_shape=parts,
            in_specs=[SMEM, VMEM, VMEM, VMEM, VMEM, VMEM],
            out_specs=VMEM,
            scratch_shapes=[pltpu.VMEM(parts.shape, jnp.bfloat16)],
            cost_estimate=cost(
                ATTEND_WEIGHT * 2 * queries.shape[0] * queries.shape[1] * 5 * tokens, 2 << 20
            ),
            compiler_params=pltpu.CompilerParams(vmem_limit_bytes=16 << 20),
            name="attend_kept" if mine else "attend_sent",
        )(user_lengths, queries, own, near, far, partner)
        for mine in (False, True)
    ]
    arrived = lax.ppermute(sent, "half", swap)
    pairs = pl.pallas_call(
        pair_kernel,
        out_shape=(pair,) * quarters,
        in_specs=[VMEM, VMEM],
        out_specs=(VMEM,) * quarters,
        cost_estimate=cost(0, tokens * queries.shape[1] * 4),
        compiler_params=pltpu.CompilerParams(vmem_limit_bytes=4 << 20),
        name="pair",
    )(kept, arrived)
    gathered = [pairs[0]] + [
        lax.ppermute(pairs[e], "quarter", [(i, i ^ e) for i in range(quarters)])
        for e in range(1, quarters)
    ]
    kv_cache = pl.pallas_call(
        collect_kernel,
        out_shape=jax.ShapeDtypeStruct((pages,) + page_block, jnp.bfloat16),
        in_specs=[SMEM, VMEM],
        out_specs=VMEM,
        cost_estimate=cost(0, pages * PAGE_ROWS * kv_width * 8),
        compiler_params=pltpu.CompilerParams(vmem_limit_bytes=4 << 20),
        name="collect",
    )(source, incoming)
    gathered[-1], kv_cache = lax.optimization_barrier((gathered[-1], kv_cache))
    attention_out = pl.pallas_call(
        join_kernel,
        out_shape=jax.ShapeDtypeStruct(
            (part_rows, HALVES * quarters * queries.shape[1]), jnp.bfloat16
        ),
        in_specs=[VMEM] * quarters,
        out_specs=VMEM,
        cost_estimate=cost(0, tokens * queries.shape[1] * 4),
        compiler_params=pltpu.CompilerParams(vmem_limit_bytes=4 << 20),
        name="join",
    )(*gathered)

    return attention_out, kv_cache


def solution(mesh):
    x, z, y = 4, 8, mesh.shape["head"]
    chips = mesh.shape["slab"] // CORES
    z = next(n for n in (8, 4, 2, 1) if chips % n == 0)
    x = chips // z
    axes = ("x", "z", "core", "half", "quarter")
    split = Mesh(mesh.devices.reshape(x, z, CORES, HALVES, y // HALVES), axes)
    slab, head = axes[:3], axes[3:]
    return jax.shard_map(
        body,
        mesh=split,
        in_specs=(P(slab, head), P(slab, head), P(slab, head), P(), P()),
        out_specs=(P(slab + head, None), P(slab, None, None, head)),
        check_vma=False,
    )
```

```python
import functools

import jax
import jax.numpy as jnp
from jax import lax
from jax.experimental import pallas as pl
from jax.experimental.pallas import tpu as pltpu
from jax.sharding import Mesh
from jax.sharding import PartitionSpec as P

HEAD_DIM = 128
WINDOW = 1024
PAGE_ROWS = 16
QUERY_SCALE = 168.0 ** (-0.5)
LOG2_E = 1.4426950408889634
MASKED = -1e30
CORES = 2
HALVES = 2
ATTEND_WEIGHT = 17

VMEM = pl.BlockSpec(memory_space=pltpu.VMEM)
SMEM = pl.BlockSpec(memory_space=pltpu.SMEM)
ANY = pl.BlockSpec(memory_space=pl.ANY)


def user_first(positions, lengths_ref):
    first = jnp.zeros_like(positions)
    start = jnp.int32(0)
    for user in range(lengths_ref.shape[0]):
        first = jnp.where(positions >= start, start, first)
        start = start + lengths_ref[user]
    return first


def user_last(positions, lengths_ref):
    ends = []
    end = jnp.int32(0)
    for user in range(lengths_ref.shape[0]):
        end = end + lengths_ref[user]
        ends.append(end)
    last = jnp.zeros_like(positions) + ends[-1]
    for end in reversed(ends[:-1]):
        last = jnp.where(positions < end, end, last)
    return last


def here():
    core = lax.axis_index("core")
    chip = lax.axis_index("x") * lax.axis_size("z") + lax.axis_index("z")
    return chip * CORES + core, core


def prepare_kernel(lengths_ref, slot_ref, keys_ref, values_ref, out_ref, live_ref, sems):
    slab, _ = here()
    tokens, kv_width = keys_ref.shape
    pages = tokens // PAGE_ROWS
    copies = []
    for page in range(pages):
        rows = slice(page * PAGE_ROWS, (page + 1) * PAGE_ROWS)
        positions = (slab * pages + page) * PAGE_ROWS + lax.broadcasted_iota(
            jnp.int32, (PAGE_ROWS, kv_width), 0
        )
        live = positions >= user_last(positions, lengths_ref) - WINDOW
        for side, ref in enumerate((keys_ref, values_ref)):
            live_ref[page, side] = jnp.where(live, ref[rows, :], 0).astype(live_ref.dtype)
        owner = slot_ref[slab * pages + page] // pages
        copies.append(pltpu.make_async_copy(live_ref.at[page], out_ref.at[owner], sems.at[page]))
        copies[-1].start()
    for copy in copies:
        copy.wait()


def collect_kernel(source_ref, in_ref, out_ref):
    for slot in range(out_ref.shape[0]):
        out_ref[slot] = in_ref[source_ref[slot]]


def attend_kernel(
    mine, lengths_ref, queries_ref, own_ref, near_ref, far_ref, partner_ref, out_ref, parts_ref
):
    slab, core = here()
    tokens = queries_ref.shape[0]
    kv_local = own_ref.shape[2] // HEAD_DIM
    group = queries_ref.shape[1] // (kv_local * HEAD_DIM)
    first_core = core == 0
    half, quarter = lax.axis_index("half"), lax.axis_index("quarter")
    quarters, part_rows = out_ref.shape[:2]
    rows = quarters * part_rows
    block_half = half if mine else 1 - half
    pieces = [
        (own_ref, 0),
        (near_ref, 2),
        (far_ref, 4),
        (partner_ref.at[0], jnp.where(first_core, 1, 3)),
        (partner_ref.at[1], jnp.where(first_core, 3, 1)),
    ]
    place = lax.broadcasted_iota(jnp.int32, (group * rows, 1), 0) % rows
    row = (place // part_rows * HALVES + block_half) * part_rows + place % part_rows
    column = lax.broadcasted_iota(jnp.int32, (group * rows, tokens), 1)
    first = user_first(slab * tokens + row, lengths_ref)
    causal = column <= row
    for g in range(kv_local):
        kv_columns = slice(g * HEAD_DIM, (g + 1) * HEAD_DIM)
        heads = range(g * group, (g + 1) * group)
        query = jnp.concatenate(
            [
                queries_ref[
                    pl.ds((target * HALVES + block_half) * part_rows, part_rows),
                    h * HEAD_DIM : (h + 1) * HEAD_DIM,
                ]
                for h in heads
                for target in range(quarters)
            ]
        )
        scores = []
        for ref, back in pieces:
            s = lax.dot_general(
                query,
                ref[0, :, kv_columns],
                (((1,), (1,)), ((), ())),
                preferred_element_type=jnp.float32,
            )
            begin = first - (slab - back) * tokens
            if ref is far_ref:
                begin = jnp.maximum(begin, row + 1)
            allowed = column >= begin
            if ref is own_ref:
                allowed = allowed & causal
            scores.append(jnp.where(allowed, s, MASKED))
        peak = functools.reduce(jnp.maximum, scores)
        row_max = jnp.max(peak, axis=1, keepdims=True)
        total, mixed = None, None
        for (ref, back), s in zip(pieces, scores):
            shifted = jnp.exp2((s - row_max) * (QUERY_SCALE * LOG2_E))
            part = jnp.dot(
                shifted.astype(jnp.bfloat16),
                ref[1, :, kv_columns],
                preferred_element_type=jnp.float32,
            )
            total = shifted if total is None else total + shifted
            mixed = part if mixed is None else mixed + part
        denominators = jnp.sum(total, axis=1, keepdims=True)
        result = (mixed / denominators).astype(out_ref.dtype)
        for r, h in enumerate(heads):
            for target in range(quarters):
                start = r * rows + target * part_rows
                parts_ref[target, :, h * HEAD_DIM : (h + 1) * HEAD_DIM] = result[
                    start : start + part_rows
                ]
    for e in range(quarters):
        out_ref[e] = parts_ref[quarter ^ e]


def pair_kernel(kept_ref, arrived_ref, *out_refs):
    half = lax.axis_index("half")
    for e, ref in enumerate(out_refs):
        ref[half] = kept_ref[e]
        ref[1 - half] = arrived_ref[e]


def join_kernel(*refs):
    *in_refs, out_ref = refs
    quarter = lax.axis_index("quarter")
    width = in_refs[0].shape[2]
    for e, ref in enumerate(in_refs):
        for half in range(HALVES):
            start = ((quarter ^ e) * HALVES + half) * width
            out_ref[:, pl.ds(pl.multiple_of(start, width), width)] = ref[half]


def cost(flops, moved):
    return pl.CostEstimate(flops=flops, bytes_accessed=moved, transcendentals=0)


def body(queries, keys, values, user_lengths, page_slot):
    slab_axes = ("x", "z", "core")
    tokens, kv_width = keys.shape
    slabs = page_slot.shape[0] // (tokens // PAGE_ROWS)
    pages = tokens // PAGE_ROWS
    slab = lax.axis_index(slab_axes)
    core = lax.axis_index("core")

    page_block = (2, PAGE_ROWS, kv_width)
    own = jnp.stack([keys, values])
    outgoing = pl.pallas_call(
        prepare_kernel,
        out_shape=jax.ShapeDtypeStruct((slabs,) + page_block, jnp.bfloat16),
        in_specs=[SMEM, SMEM, VMEM, VMEM],
        out_specs=ANY,
        scratch_shapes=[
            pltpu.VMEM((pages,) + page_block, jnp.bfloat16),
            pltpu.SemaphoreType.DMA((pages,)),
        ],
        cost_estimate=cost(0, pages * PAGE_ROWS * kv_width * 16),
        name="prepare",
    )(user_lengths, page_slot, keys, values)
    chips = lax.axis_size("x") * lax.axis_size("z")
    forward = [(i, i + 1) for i in range(chips - 1)]
    near = lax.ppermute(own, ("x", "z"), forward)
    near, outgoing = lax.optimization_barrier((near, outgoing))
    far = lax.ppermute(near, ("x", "z"), forward)
    incoming = lax.all_to_all(outgoing, slab_axes, split_axis=0, concat_axis=0, tiled=True)
    given = jnp.stack([near, jnp.where(core == 0, own, far)])
    swap = [(0, 1), (1, 0)]
    partner = lax.ppermute(given, "core", swap)

    slots = slab * pages + jnp.arange(pages, dtype=jnp.int32)
    page_index = jnp.arange(page_slot.shape[0], dtype=jnp.int32)
    source = jnp.sum(
        jnp.where(page_slot[None, :] == slots[:, None], page_index[None, :] // pages, 0), axis=1
    )

    quarters = lax.axis_size("quarter")
    part_rows = tokens // (HALVES * quarters)
    parts = jax.ShapeDtypeStruct((quarters, part_rows, queries.shape[1]), jnp.bfloat16)
    pair = jax.ShapeDtypeStruct((HALVES,) + parts.shape[1:], jnp.bfloat16)
    sent, kept = [
        pl.pallas_call(
            functools.partial(attend_kernel, mine),
            out_shape=parts,
            in_specs=[SMEM, VMEM, VMEM, VMEM, VMEM, VMEM],
            out_specs=VMEM,
            scratch_shapes=[pltpu.VMEM(parts.shape, jnp.bfloat16)],
            cost_estimate=cost(
                ATTEND_WEIGHT * 2 * queries.shape[0] * queries.shape[1] * 5 * tokens, 2 << 20
            ),
            compiler_params=pltpu.CompilerParams(vmem_limit_bytes=16 << 20),
            name="attend_kept" if mine else "attend_sent",
        )(user_lengths, queries, own, near, far, partner)
        for mine in (False, True)
    ]
    arrived = lax.ppermute(sent, "half", swap)
    pairs = pl.pallas_call(
        pair_kernel,
        out_shape=(pair,) * quarters,
        in_specs=[VMEM, VMEM],
        out_specs=(VMEM,) * quarters,
        cost_estimate=cost(0, tokens * queries.shape[1] * 4),
        compiler_params=pltpu.CompilerParams(vmem_limit_bytes=4 << 20),
        name="pair",
    )(kept, arrived)
    gathered = [pairs[0]] + [
        lax.ppermute(pairs[e], "quarter", [(i, i ^ e) for i in range(quarters)])
        for e in range(1, quarters)
    ]
    kv_cache = pl.pallas_call(
        collect_kernel,
        out_shape=jax.ShapeDtypeStruct((pages,) + page_block, jnp.bfloat16),
        in_specs=[SMEM, VMEM],
        out_specs=VMEM,
        cost_estimate=cost(0, pages * PAGE_ROWS * kv_width * 8),
        compiler_params=pltpu.CompilerParams(vmem_limit_bytes=4 << 20),
        name="collect",
    )(source, incoming)
    gathered[-1], kv_cache = lax.optimization_barrier((gathered[-1], kv_cache))
    attention_out = pl.pallas_call(
        join_kernel,
        out_shape=jax.ShapeDtypeStruct(
            (part_rows, HALVES * quarters * queries.shape[1]), jnp.bfloat16
        ),
        in_specs=[VMEM] * quarters,
        out_specs=VMEM,
        cost_estimate=cost(0, tokens * queries.shape[1] * 4),
        compiler_params=pltpu.CompilerParams(vmem_limit_bytes=4 << 20),
        name="join",
    )(*gathered)

    return attention_out, kv_cache


def solution(mesh):
    x, z, y = 4, 8, mesh.shape["head"]
    chips = mesh.shape["slab"] // CORES
    z = next(n for n in (8, 4, 2, 1) if chips % n == 0)
    x = chips // z
    axes = ("x", "z", "core", "quarter", "half")
    split = Mesh(mesh.devices.reshape(x, z, CORES, y // HALVES, HALVES), axes)
    slab, head = axes[:3], axes[3:]
    return jax.shard_map(
        body,
        mesh=split,
        in_specs=(P(slab, head), P(slab, head), P(slab, head), P(), P()),
        out_specs=(P(slab + head, None), P(slab, None, None, head)),
        check_vma=False,
    )
```

```python
import functools

import jax
import jax.numpy as jnp
from jax import lax
from jax.experimental import pallas as pl
from jax.experimental.pallas import tpu as pltpu
from jax.sharding import Mesh
from jax.sharding import PartitionSpec as P

HEAD_DIM = 128
WINDOW = 1024
PAGE_ROWS = 16
QUERY_SCALE = 168.0 ** (-0.5)
LOG2_E = 1.4426950408889634
MASKED = -1e30
CORES = 2
HALVES = 2
ATTEND_WEIGHT = 17

VMEM = pl.BlockSpec(memory_space=pltpu.VMEM)
SMEM = pl.BlockSpec(memory_space=pltpu.SMEM)
ANY = pl.BlockSpec(memory_space=pl.ANY)


def user_first(positions, lengths_ref):
    first = jnp.zeros_like(positions)
    start = jnp.int32(0)
    for user in range(lengths_ref.shape[0]):
        first = jnp.where(positions >= start, start, first)
        start = start + lengths_ref[user]
    return first


def user_last(positions, lengths_ref):
    ends = []
    end = jnp.int32(0)
    for user in range(lengths_ref.shape[0]):
        end = end + lengths_ref[user]
        ends.append(end)
    last = jnp.zeros_like(positions) + ends[-1]
    for end in reversed(ends[:-1]):
        last = jnp.where(positions < end, end, last)
    return last


def here():
    core = lax.axis_index("core")
    chip = lax.axis_index("x") * lax.axis_size("z") + lax.axis_index("z")
    return chip * CORES + core, core


def stack_kernel(keys_ref, values_ref, own_ref, sems):
    copies = [
        pltpu.make_async_copy(ref, own_ref.at[side], sems.at[side])
        for side, ref in enumerate((keys_ref, values_ref))
    ]
    for copy in copies:
        copy.start()
    for copy in copies:
        copy.wait()


def prepare_kernel(lengths_ref, slot_ref, keys_ref, values_ref, out_ref, live_ref, sems):
    slab, _ = here()
    tokens, kv_width = keys_ref.shape
    pages = tokens // PAGE_ROWS
    copies = []
    for page in range(pages):
        rows = slice(page * PAGE_ROWS, (page + 1) * PAGE_ROWS)
        positions = (slab * pages + page) * PAGE_ROWS + lax.broadcasted_iota(
            jnp.int32, (PAGE_ROWS, kv_width), 0
        )
        live = positions >= user_last(positions, lengths_ref) - WINDOW
        for side, ref in enumerate((keys_ref, values_ref)):
            live_ref[page, side] = jnp.where(live, ref[rows, :], 0).astype(live_ref.dtype)
        owner = slot_ref[slab * pages + page] // pages
        copies.append(pltpu.make_async_copy(live_ref.at[page], out_ref.at[owner], sems.at[page]))
        copies[-1].start()
    for copy in copies:
        copy.wait()


def collect_kernel(source_ref, in_ref, out_ref):
    for slot in range(out_ref.shape[0]):
        out_ref[slot] = in_ref[source_ref[slot]]


def attend_kernel(
    mine, lengths_ref, queries_ref, own_ref, near_ref, far_ref, partner_ref, out_ref, parts_ref
):
    slab, core = here()
    tokens = queries_ref.shape[0]
    kv_local = own_ref.shape[2] // HEAD_DIM
    group = queries_ref.shape[1] // (kv_local * HEAD_DIM)
    first_core = core == 0
    half, quarter = lax.axis_index("half"), lax.axis_index("quarter")
    quarters, part_rows = out_ref.shape[:2]
    rows = quarters * part_rows
    block_half = half if mine else 1 - half
    pieces = [
        (own_ref, 0),
        (near_ref, 2),
        (far_ref, 4),
        (partner_ref.at[0], jnp.where(first_core, 1, 3)),
        (partner_ref.at[1], jnp.where(first_core, 3, 1)),
    ]
    place = lax.broadcasted_iota(jnp.int32, (group * rows, 1), 0) % rows
    row = (place // part_rows * HALVES + block_half) * part_rows + place % part_rows
    column = lax.broadcasted_iota(jnp.int32, (group * rows, tokens), 1)
    first = user_first(slab * tokens + row, lengths_ref)
    causal = column <= row
    for g in range(kv_local):
        kv_columns = slice(g * HEAD_DIM, (g + 1) * HEAD_DIM)
        heads = range(g * group, (g + 1) * group)
        query = jnp.concatenate(
            [
                queries_ref[
                    pl.ds((target * HALVES + block_half) * part_rows, part_rows),
                    h * HEAD_DIM : (h + 1) * HEAD_DIM,
                ]
                for h in heads
                for target in range(quarters)
            ]
        )
        scores = []
        for ref, back in pieces:
            s = lax.dot_general(
                query,
                ref[0, :, kv_columns],
                (((1,), (1,)), ((), ())),
                preferred_element_type=jnp.float32,
            )
            begin = first - (slab - back) * tokens
            if ref is far_ref:
                begin = jnp.maximum(begin, row + 1)
            allowed = column >= begin
            if ref is own_ref:
                allowed = allowed & causal
            scores.append(jnp.where(allowed, s, MASKED))
        peak = functools.reduce(jnp.maximum, scores)
        row_max = jnp.max(peak, axis=1, keepdims=True)
        total, mixed = None, None
        for (ref, back), s in zip(pieces, scores):
            shifted = jnp.exp2((s - row_max) * (QUERY_SCALE * LOG2_E))
            part = jnp.dot(
                shifted.astype(jnp.bfloat16),
                ref[1, :, kv_columns],
                preferred_element_type=jnp.float32,
            )
            total = shifted if total is None else total + shifted
            mixed = part if mixed is None else mixed + part
        denominators = jnp.sum(total, axis=1, keepdims=True)
        result = (mixed / denominators).astype(out_ref.dtype)
        for r, h in enumerate(heads):
            for target in range(quarters):
                start = r * rows + target * part_rows
                parts_ref[target, :, h * HEAD_DIM : (h + 1) * HEAD_DIM] = result[
                    start : start + part_rows
                ]
    for e in range(quarters):
        out_ref[e] = parts_ref[quarter ^ e]


def pair_kernel(kept_ref, arrived_ref, *out_refs):
    half = lax.axis_index("half")
    for e, ref in enumerate(out_refs):
        ref[half] = kept_ref[e]
        ref[1 - half] = arrived_ref[e]


def join_kernel(*refs):
    *in_refs, out_ref = refs
    quarter = lax.axis_index("quarter")
    width = in_refs[0].shape[2]
    for e, ref in enumerate(in_refs):
        for half in range(HALVES):
            start = ((quarter ^ e) * HALVES + half) * width
            out_ref[:, pl.ds(pl.multiple_of(start, width), width)] = ref[half]


def cost(flops, moved):
    return pl.CostEstimate(flops=flops, bytes_accessed=moved, transcendentals=0)


def body(queries, keys, values, user_lengths, page_slot):
    slab_axes = ("x", "z", "core")
    tokens, kv_width = keys.shape
    slabs = page_slot.shape[0] // (tokens // PAGE_ROWS)
    pages = tokens // PAGE_ROWS
    slab = lax.axis_index(slab_axes)
    core = lax.axis_index("core")

    page_block = (2, PAGE_ROWS, kv_width)
    own = pl.pallas_call(
        stack_kernel,
        out_shape=jax.ShapeDtypeStruct((2, tokens, kv_width), jnp.bfloat16),
        in_specs=[ANY, ANY],
        out_specs=VMEM,
        scratch_shapes=[pltpu.SemaphoreType.DMA((2,))],
        cost_estimate=cost(0, tokens * kv_width * 8),
        compiler_params=pltpu.CompilerParams(vmem_limit_bytes=4 << 20),
        name="stack",
    )(keys, values)
    outgoing = pl.pallas_call(
        prepare_kernel,
        out_shape=jax.ShapeDtypeStruct((slabs,) + page_block, jnp.bfloat16),
        in_specs=[SMEM, SMEM, VMEM, VMEM],
        out_specs=ANY,
        scratch_shapes=[
            pltpu.VMEM((pages,) + page_block, jnp.bfloat16),
            pltpu.SemaphoreType.DMA((pages,)),
        ],
        cost_estimate=cost(0, pages * PAGE_ROWS * kv_width * 16),
        name="prepare",
    )(user_lengths, page_slot, keys, values)
    chips = lax.axis_size("x") * lax.axis_size("z")
    forward = [(i, i + 1) for i in range(chips - 1)]
    near = lax.ppermute(own, ("x", "z"), forward)
    near, outgoing = lax.optimization_barrier((near, outgoing))
    far = lax.ppermute(near, ("x", "z"), forward)
    incoming = lax.all_to_all(outgoing, slab_axes, split_axis=0, concat_axis=0, tiled=True)
    given = jnp.stack([near, jnp.where(core == 0, own, far)])
    swap = [(0, 1), (1, 0)]
    partner = lax.ppermute(given, "core", swap)

    slots = slab * pages + jnp.arange(pages, dtype=jnp.int32)
    page_index = jnp.arange(page_slot.shape[0], dtype=jnp.int32)
    source = jnp.sum(
        jnp.where(page_slot[None, :] == slots[:, None], page_index[None, :] // pages, 0), axis=1
    )

    quarters = lax.axis_size("quarter")
    part_rows = tokens // (HALVES * quarters)
    parts = jax.ShapeDtypeStruct((quarters, part_rows, queries.shape[1]), jnp.bfloat16)
    pair = jax.ShapeDtypeStruct((HALVES,) + parts.shape[1:], jnp.bfloat16)
    sent, kept = [
        pl.pallas_call(
            functools.partial(attend_kernel, mine),
            out_shape=parts,
            in_specs=[SMEM, VMEM, VMEM, VMEM, VMEM, VMEM],
            out_specs=VMEM,
            scratch_shapes=[pltpu.VMEM(parts.shape, jnp.bfloat16)],
            cost_estimate=cost(
                ATTEND_WEIGHT * 2 * queries.shape[0] * queries.shape[1] * 5 * tokens, 2 << 20
            ),
            compiler_params=pltpu.CompilerParams(vmem_limit_bytes=16 << 20),
            name="attend_kept" if mine else "attend_sent",
        )(user_lengths, queries, own, near, far, partner)
        for mine in (False, True)
    ]
    arrived = lax.ppermute(sent, "half", swap)
    pairs = pl.pallas_call(
        pair_kernel,
        out_shape=(pair,) * quarters,
        in_specs=[VMEM, VMEM],
        out_specs=(VMEM,) * quarters,
        cost_estimate=cost(0, tokens * queries.shape[1] * 4),
        compiler_params=pltpu.CompilerParams(vmem_limit_bytes=4 << 20),
        name="pair",
    )(kept, arrived)
    gathered = [pairs[0]] + [
        lax.ppermute(pairs[e], "quarter", [(i, i ^ e) for i in range(quarters)])
        for e in range(1, quarters)
    ]
    kv_cache = pl.pallas_call(
        collect_kernel,
        out_shape=jax.ShapeDtypeStruct((pages,) + page_block, jnp.bfloat16),
        in_specs=[SMEM, VMEM],
        out_specs=VMEM,
        cost_estimate=cost(0, pages * PAGE_ROWS * kv_width * 8),
        compiler_params=pltpu.CompilerParams(vmem_limit_bytes=4 << 20),
        name="collect",
    )(source, incoming)
    gathered[-1], kv_cache = lax.optimization_barrier((gathered[-1], kv_cache))
    attention_out = pl.pallas_call(
        join_kernel,
        out_shape=jax.ShapeDtypeStruct(
            (part_rows, HALVES * quarters * queries.shape[1]), jnp.bfloat16
        ),
        in_specs=[VMEM] * quarters,
        out_specs=VMEM,
        cost_estimate=cost(0, tokens * queries.shape[1] * 4),
        compiler_params=pltpu.CompilerParams(vmem_limit_bytes=4 << 20),
        name="join",
    )(*gathered)

    return attention_out, kv_cache


def solution(mesh):
    x, z, y = 4, 8, mesh.shape["head"]
    chips = mesh.shape["slab"] // CORES
    z = next(n for n in (8, 4, 2, 1) if chips % n == 0)
    x = chips // z
    axes = ("x", "z", "core", "quarter", "half")
    split = Mesh(mesh.devices.reshape(x, z, CORES, y // HALVES, HALVES), axes)
    slab, head = axes[:3], axes[3:]
    return jax.shard_map(
        body,
        mesh=split,
        in_specs=(P(slab, head), P(slab, head), P(slab, head), P(), P()),
        out_specs=(P(slab + head, None), P(slab, None, None, head)),
        check_vma=False,
    )
```
